512 devices in a mesh: seq: 8 (over z), dec: 32 (over y, x), rep: 2 (over core).
Axes of the slice: x: 4, y: 8, z: 8, core: 2. Of those that a mesh axis runs over, the one named last changes fastest.
Arguments:
- queries: bfloat16 [64, 128, 8192], P(('rep', 'dec'), 'seq'), parts along dimension 0, may hold values from -360 to 360
- slab_kv: bfloat16 [64, 128, 2048], P(('rep', 'dec'), 'seq'), parts along dimension 0, may hold values from -6 to 6
- prefix_kv: bfloat16 [2048, 2048], P(('rep', 'dec'), 'seq'), parts along dimension 0, may hold values from -6 to 6
- owners: int32 [16, 32], P(('rep', 'seq')), parts along dimension 0, may hold values from 0 to 31, as said below
- offset: int32 [2], P('rep'), parts along dimension 0, may hold values from 512 to 1024
Outputs:
- attention: bfloat16 [64, 128, 8192], P(('rep', 'dec'), 'seq'), parts along dimension 0
- page_store: bfloat16 [16, 32, 2, 128, 256], P(('rep', 'seq'), 'dec'), parts along dimension 0
- page_scales: bfloat16 [16, 32, 2, 2], P(('rep', 'seq'), 'dec'), parts along dimension 0
The draws below stay inside these ranges and needn't reach their ends.
There are 2 independent parts, one for each index of `rep`. The reference program is written for one: setup_inputs(seed, part) draws one part's arguments, and reference() takes and returns one part's arrays. A program takes and returns all parts, laid end to end along the dimension named above; each array names one. Nothing has to cross between parts.
Inputs may be any that keep to these rules, and one draw needn't show every extreme that they name: `owners`: for each head no owner holds more than 2 pages, and some owner holds exactly 2 pages of every head.
All inputs are finite; a program needn't handle non-finite values. Where the reference program divides by a largest or mean magnitude, that divisor is 1e-20 or more.
Results may differ from the reference program's by a relative error of at most 0.025.
The reference program's roundings to bfloat16 on the way count: a program that leaves them out, or rounds other values in their place, can miss the bound.
Values may be sent and summed in bfloat16 or wider, within the bound.
No kernel may reach another device: no remote copies, remote signals or barrier semaphores. Data moves between devices by JAX's collectives and lax.ppermute only.
A program may use at most 64 MiB of HBM per device.

```python
import jax
import jax.numpy as jnp
from jax import lax

HQ = 64
KVH = 8
HD = 128
PAGE = 128
QROWS = 128
BLOCKS = 32
PREFIX = 1024
PAGES = 32
SLOTS = 2


def draw_queries(key, part):
    key = jax.random.fold_in(key, 11)
    base = jnp.clip(jax.random.normal(key, (BLOCKS, QROWS, HQ, HD), jnp.float32), -6.0, 6.0)
    return base.reshape(BLOCKS, QROWS, HQ * HD).astype(jnp.bfloat16)


def owner_row(key):
    filled = jax.random.randint(jax.random.fold_in(key, 1), (), 0, BLOCKS)
    spare = jax.random.permutation(jax.random.fold_in(key, 2), (BLOCKS - 1) * SLOTS)[:PAGES - SLOTS] // SLOTS
    spare = spare + (spare >= filled).astype(jnp.int32)
    listing = jnp.concatenate([jnp.full((SLOTS,), filled, jnp.int32), spare.astype(jnp.int32)])
    return jax.random.permutation(jax.random.fold_in(key, 3), listing)


def draw_owners(key, part):
    key = jax.random.fold_in(key, 23)
    keys = jax.random.split(key, KVH)
    return jax.vmap(owner_row)(keys).astype(jnp.int32)


def block_scale(rng, shape, shards, low, high):
    def one(dim, parts):
        draws = jax.random.uniform(jax.random.fold_in(jax.random.fold_in(rng, 6), dim), (parts,), jnp.float32, low / len(shards), high / len(shards))
        return jnp.repeat(jnp.exp(draws), shape[dim] // parts).reshape((-1,) + (1,) * (len(shape) - dim - 1))

    gain = one(*shards[0])
    for cut in shards[1:]:
        gain = gain * one(*cut)
    return gain


def normal_values(stream_key, dims, scale, most, pieces=(), kind=jnp.bfloat16):
    result = scale * jax.random.normal(stream_key, dims, jnp.float32)
    if pieces:
        result = result * block_scale(stream_key, dims, pieces, -0.22, 0.18)
    return jnp.clip(result, -most, most).astype(kind)


def setup_inputs(seed: int = 0, part: int = 0) -> dict:
    arg_keys = jax.random.split(jax.random.key(seed), 6)
    own_keys = jax.random.split(jax.random.fold_in(arg_keys[5], part), 6)
    return {
        "queries": draw_queries(jax.random.fold_in(jax.random.fold_in(arg_keys[5], part), 71), part),
        "slab_kv": normal_values(own_keys[1], (BLOCKS, QROWS, KVH * 2 * HD), 1.0, 6.0, ((0, 32), (1, 8))),
        "prefix_kv": normal_values(own_keys[2], (PREFIX, KVH * 2 * HD), 1.0, 6.0, ((0, 32), (1, 8))),
        "owners": draw_owners(jax.random.fold_in(jax.random.fold_in(arg_keys[5], part), 71), part),
        "offset": jax.random.randint(own_keys[4], (1,), PREFIX // 2, PREFIX + 1).astype(jnp.int32),
    }


rope_base = 1000000.0
tiny = 1e-6
masked = -1e30


def rotate(values, position):
    width = values.shape[-1]
    middle = width // 2
    inverse = rope_base ** (-(jnp.arange(middle, dtype=jnp.float32) * 2.0 / width))
    angles = position.astype(jnp.float32)[:, None] * inverse[None, :]
    cosine = jnp.cos(angles)[:, None, :]
    sinus = jnp.sin(angles)[:, None, :]
    leading = values[..., :middle].astype(jnp.float32)
    trailing = values[..., middle:].astype(jnp.float32)
    return jnp.concatenate([leading * cosine - trailing * sinus, trailing * cosine + leading * sinus], axis=-1)


def quantize(rows_kv, heads, width, page_len):
    number = rows_kv.shape[0] // page_len
    grouped = rows_kv.reshape(number, page_len, heads, 2, width).astype(jnp.float32)
    largest = jnp.max(jnp.abs(grouped), axis=(1, 4))
    scaled = (grouped / (largest[:, None, :, :, None] + tiny)).astype(jnp.bfloat16)
    scaled = scaled.transpose(2, 0, 1, 3, 4).reshape(heads, number, page_len * 2 * width)
    return scaled, largest.transpose(1, 0, 2).astype(jnp.bfloat16)


def page_ranks(targets):
    number = targets.shape[1]
    matching = targets[:, :, None] == targets[:, None, :]
    indices = jnp.arange(number, dtype=jnp.int32)
    earlier = indices[:, None] > indices[None, :]
    return jnp.sum((matching & earlier[None]).astype(jnp.int32), axis=2).astype(jnp.int32)


def reference(queries, slab_kv, prefix_kv, owners, offset):
    total = BLOCKS * QROWS
    group = HQ // KVH
    begin = offset[0].astype(jnp.int32)
    slab_index = jnp.arange(total, dtype=jnp.int32)
    position = begin + slab_index
    turned = rotate(queries.reshape(total, HQ, HD), position).astype(jnp.bfloat16)
    paired = slab_kv.reshape(total, KVH, 2, HD)
    fresh_keys = rotate(paired[:, :, 0], position).astype(jnp.bfloat16)
    fresh_values = paired[:, :, 1]
    cached = prefix_kv.reshape(PREFIX, KVH, 2, HD)
    prefix_open = jnp.arange(PREFIX, dtype=jnp.int32) < begin
    scale = HD ** -0.5

    def head_output(head):
        key_rows = jnp.concatenate([cached[:, head, 0], fresh_keys[:, head]], axis=0).astype(jnp.float32)
        value_rows = jnp.concatenate([cached[:, head, 1], fresh_values[:, head]], axis=0).astype(jnp.float32)
        asking = lax.dynamic_slice_in_dim(turned, (head * group).astype(jnp.int32), group, 1)
        asking = asking.reshape(BLOCKS, QROWS, group, HD)

        def block_output(inputs):
            block_queries, block_first = inputs
            query_index = block_first + jnp.arange(QROWS, dtype=jnp.int32)
            allowed = jnp.concatenate([jnp.broadcast_to(prefix_open[None, :], (QROWS, PREFIX)), slab_index[None, :] <= query_index[:, None]], axis=1)
            scores = jnp.einsum("tgd,nd->tgn", block_queries.astype(jnp.float32), key_rows) * scale
            scores = jnp.where(allowed[:, None, :], scores, masked)
            highest = jnp.max(scores, axis=-1, keepdims=True)
            weights = jnp.where(allowed[:, None, :], jnp.exp(scores - highest), 0.0)
            rounded = lax.optimization_barrier(weights.astype(jnp.bfloat16))
            numer = jnp.einsum("tgn,nd->tgd", rounded.astype(jnp.float32), value_rows)
            return (numer / jnp.sum(weights, axis=-1, keepdims=True)).astype(jnp.bfloat16)

        return lax.map(block_output, (asking, jnp.arange(BLOCKS, dtype=jnp.int32) * QROWS))

    per_head = lax.map(head_output, jnp.arange(KVH, dtype=jnp.int32))
    attention = per_head.transpose(1, 2, 0, 3, 4).reshape(BLOCKS, QROWS, HQ * HD)
    fresh_pairs = jnp.stack([fresh_keys, fresh_values], axis=2).reshape(total, KVH * 2 * HD)
    page_values, page_tops = quantize(fresh_pairs, KVH, HD, PAGE)
    ranks_all = page_ranks(owners)
    head_index = jnp.broadcast_to(jnp.arange(KVH, dtype=jnp.int32)[:, None], owners.shape)
    stored = jnp.zeros((KVH, BLOCKS, SLOTS, PAGE * 2 * HD), jnp.bfloat16).at[head_index, owners, ranks_all].set(page_values)
    tops = jnp.zeros((KVH, BLOCKS, SLOTS, 2), jnp.bfloat16).at[head_index, owners, ranks_all].set(page_tops)
    return attention, stored.reshape(KVH, BLOCKS, SLOTS, PAGE, 2 * HD), tops
```

```python
import functools
import math

import jax
import jax.numpy as jnp
import numpy as np
from jax import lax
from jax.experimental import pallas as pl
from jax.experimental.pallas import tpu as pltpu
from jax.sharding import Mesh, PartitionSpec as P

HQ = 64
KVH = 8
HD = 128
PAGE = 128
GROUP = HQ // KVH
TOK = 16
WIDE = 2 * HD
NX = 4

rope_base = 1000000.0
tiny = 1e-06
masked = -1e30
to_exp2 = HD ** (-0.5) * math.log2(math.e)

VMEM = pltpu.VMEM
SMEM = pltpu.SMEM


def spec(space=VMEM):
    return pl.BlockSpec(memory_space=space)


def params(mib=48):
    return pltpu.CompilerParams(vmem_limit_bytes=mib * 1024 * 1024)


def turn(x, cosine, sinus):
    x = x.astype(jnp.float32)
    return (x * cosine + pltpu.roll(x, HD // 2, 1) * sinus).astype(jnp.bfloat16)


def pack_kv(pos_ref, inv_ref, kv_ref, out_ref, cos_ref, sin_ref):
    row = lax.broadcasted_iota(jnp.int32, (TOK, HD), 0) + pos_ref[0]
    angles = row.astype(jnp.float32) * inv_ref[...]
    lane = lax.broadcasted_iota(jnp.int32, (TOK, HD), 1)
    cosine = jnp.cos(angles)
    sinus = jnp.sin(angles)
    sinus = jnp.where(lane < HD // 2, -sinus, sinus)
    cos_ref[...] = cosine
    sin_ref[...] = sinus
    for h in range(KVH):
        key = turn(kv_ref[:, h * WIDE : h * WIDE + HD], cosine, sinus)
        value = kv_ref[:, h * WIDE + HD : (h + 1) * WIDE]
        for y in range(out_ref.shape[1]):
            out_ref[h, y, :, :HD] = key
            out_ref[h, y, :, HD:] = value


def pack_q(cos_ref, sin_ref, q_ref, out_ref):
    cosine = cos_ref[...]
    sinus = sin_ref[...]
    for q in range(HQ):
        h, g = divmod(q, GROUP)
        out_ref[h, :, g * HD : (g + 1) * HD] = turn(q_ref[:, q * HD : (q + 1) * HD], cosine, sinus)


def scores_of(q, k):
    return lax.dot_general(q, k, (((1,), (1,)), ((), ())), preferred_element_type=jnp.float32)


def lane_sum(p):
    total = p[:, :HD]
    for i in range(1, p.shape[1] // HD):
        total = total + p[:, i * HD : (i + 1) * HD]
    return total


def attend(q_ref, k, v, m_ref, l_ref, a_ref, mask=None, first=False):
    rows = PAGE
    for g in range(GROUP):
        part = slice(g * rows, (g + 1) * rows)
        s = scores_of(q_ref[part], k)
        if mask is not None:
            s = jnp.where(mask, s, masked)
        top = jnp.max(s, axis=1, keepdims=True)
        if first:
            high = jnp.broadcast_to(top, (rows, HD))
        else:
            before = m_ref[part]
            high = jnp.maximum(before, top)
            factor = jnp.exp2((before - high) * to_exp2)
        shift = high[:, :1] * to_exp2
        p = jnp.exp2(s * to_exp2 - shift)
        add = lane_sum(p)
        num = jnp.dot(p.astype(jnp.bfloat16), v, preferred_element_type=jnp.float32)
        m_ref[part] = high
        if first:
            l_ref[part] = add
            a_ref[part] = num
        else:
            l_ref[part] = l_ref[part] * factor + add
            a_ref[part] = a_ref[part] * factor + num


def fill_q(q_in, q_ref):
    for g in range(GROUP):
        q_ref[g * PAGE : (g + 1) * PAGE] = q_in[:, :, g * HD : (g + 1) * HD].reshape(PAGE, HD)


def attend_near(place_ref, q_in, col_ref, pre_ref, m_ref, l_ref, a_ref, q_ref):
    y, begin = place_ref[0], place_ref[2]
    fill_q(q_in, q_ref)

    def block(i):
        both = col_ref[:, i].reshape(PAGE, WIDE)
        return both[:, :HD], both[:, HD:]

    row = lax.broadcasted_iota(jnp.int32, (PAGE, PAGE), 0)
    key = lax.broadcasted_iota(jnp.int32, (PAGE, PAGE), 1)
    k, v = block(y)
    attend(q_ref, k, v, m_ref, l_ref, a_ref, mask=key <= row, first=True)

    @pl.loop(0, y)
    def _(i):
        k, v = block(i)
        attend(q_ref, k, v, m_ref, l_ref, a_ref)

    span = 512
    where = lax.broadcasted_iota(jnp.int32, (PAGE, span), 1)

    @pl.loop(0, pre_ref.shape[0] // span)
    def _(i):
        both = pre_ref[pl.ds(i * span, span), :]
        attend(q_ref, both[:, :HD], both[:, HD:], m_ref, l_ref, a_ref, mask=where + i * span < begin)


def attend_far(place_ref, q_in, all_ref, m_in, l_in, a_in, out_ref, m_ref, l_ref, a_ref, q_ref):
    y, x = place_ref[0], place_ref[1]
    fill_q(q_in, q_ref)
    m_ref[...] = m_in[...]
    l_ref[...] = l_in[...]
    a_ref[...] = a_in[...]
    columns = [(x + j) % NX for j in range(1, NX)]

    @pl.loop(0, y)
    def _(i):
        both = jnp.concatenate([all_ref[c, :, i].reshape(PAGE, WIDE) for c in columns], axis=0)
        attend(q_ref, both[:, :HD], both[:, HD:], m_ref, l_ref, a_ref)

    @pl.loop(0, x)
    def _(c):
        both = all_ref[c, :, y].reshape(PAGE, WIDE)
        attend(q_ref, both[:, :HD], both[:, HD:], m_ref, l_ref, a_ref)

    for g in range(GROUP):
        part = slice(g * PAGE, (g + 1) * PAGE)
        mass = jnp.sum(l_ref[part], axis=1, keepdims=True)
        done = (a_ref[part] / mass).astype(jnp.bfloat16)
        out_ref[:, :, g * HD : (g + 1) * HD] = done.reshape(KVH, TOK, HD)


def pick_pages(place_ref, own_ref, all_ref, store_ref, scale_ref):
    me = place_ref[0] * NX + place_ref[1]
    pages = own_ref.shape[1]

    def look(i, found):
        one, two = found
        p = pages - 1 - i
        hit = own_ref[0, p] == me
        return jnp.where(hit, p, one), jnp.where(hit, one, two)

    found = lax.fori_loop(0, pages, look, (jnp.int32(pages), jnp.int32(pages)))
    tops = []
    for slot in range(2):
        page = found[slot]
        held = (page < pages).astype(jnp.float32)
        page = jnp.minimum(page, pages - 1)
        both = all_ref[page % NX, :, page // NX].reshape(PAGE, WIDE).astype(jnp.float32)
        for half in range(2):
            part = both[:, half * HD : (half + 1) * HD]
            top = jnp.max(jnp.max(jnp.abs(part), axis=0, keepdims=True), axis=1, keepdims=True)
            store_ref[slot, :, half * HD : (half + 1) * HD] = (part / (top + tiny) * held).astype(jnp.bfloat16)
            tops.append(top * held)
    row = lax.broadcasted_iota(jnp.int32, (2, 2), 0)
    col = lax.broadcasted_iota(jnp.int32, (2, 2), 1)
    upper = jnp.where(col == 0, tops[0], tops[1])
    lower = jnp.where(col == 0, tops[2], tops[3])
    scale_ref[...] = jnp.where(row == 0, upper, lower).astype(jnp.bfloat16)


def unpack_out(in_ref, out_ref):
    for h in range(KVH):
        out_ref[:, h * GROUP * HD : (h + 1) * GROUP * HD] = in_ref[h]


def shaped(shape, dtype=jnp.bfloat16):
    return jax.ShapeDtypeStruct(shape, dtype)


def on_device(queries, slab_kv, prefix_kv, owners, offset):
    ny = lax.axis_size("y")
    y, x, s = lax.axis_index("y"), lax.axis_index("x"), lax.axis_index("seq")
    begin = offset[0]
    position = (begin + (y * NX + x) * PAGE + s * TOK).reshape(1)
    place = jnp.stack([y, x, begin]).astype(jnp.int32)
    half = np.arange(HD // 2, dtype=np.float64) * 2.0 / HD
    inverse = np.tile((rope_base ** (-half)).astype(np.float32), 2)[None]

    kv_send, cosine, sinus = pl.pallas_call(
        pack_kv,
        out_shape=(shaped((KVH, ny, TOK, WIDE)), shaped((TOK, HD), jnp.float32), shaped((TOK, HD), jnp.float32)),
        in_specs=[spec(SMEM), spec(), spec()],
        out_specs=(spec(), spec(), spec()),
        compiler_params=params(),
        name="pack_kv",
    )(position, jnp.asarray(inverse), slab_kv[0])
    column = lax.all_to_all(kv_send.reshape(KVH * ny, TOK, WIDE), ("seq", "y"), 0, 0, tiled=True)

    q_send = pl.pallas_call(
        pack_q,
        out_shape=shaped((KVH, TOK, GROUP * HD)),
        in_specs=[spec()] * 3,
        out_specs=spec(),
        compiler_params=params(),
        name="pack_q",
    )(cosine, sinus, queries[0])
    q_got = lax.all_to_all(q_send, "seq", 0, 0, tiled=True)

    pre_rows = prefix_kv.shape[0]
    pre_x = lax.all_to_all(jnp.broadcast_to(prefix_kv[None], (NX, pre_rows, WIDE)), "x", 0, 0, tiled=True)
    pre_x = pre_x.reshape(1, NX * pre_rows, WIDE)
    pre_all = lax.all_to_all(jnp.broadcast_to(pre_x, (ny, NX * pre_rows, WIDE)), "y", 0, 0, tiled=True)
    pre_all = pre_all.reshape(ny * NX * pre_rows, WIDE)

    every = lax.all_to_all(
        jnp.broadcast_to(column[None], (NX, KVH * ny, TOK, WIDE)), "x", 0, 0, tiled=True
    ).reshape(NX, KVH, ny, TOK, WIDE)

    rows = GROUP * PAGE
    state = (shaped((rows, HD), jnp.float32),) * 3
    keep = [VMEM((rows, HD), jnp.float32)] * 3
    hold_q = VMEM((rows, HD), jnp.bfloat16)
    m, l, a = pl.pallas_call(
        attend_near,
        out_shape=state,
        in_specs=[spec(SMEM), spec(), spec(), spec()],
        out_specs=(spec(),) * 3,
        scratch_shapes=[hold_q],
        compiler_params=params(),
        cost_estimate=pl.CostEstimate(flops=4 * rows * HD * 2048, bytes_accessed=3 << 20, transcendentals=rows * 2048),
        name="attend_near",
    )(place, q_got, column.reshape(KVH, ny, TOK, WIDE), pre_all)
    result = pl.pallas_call(
        attend_far,
        out_shape=shaped((KVH, TOK, GROUP * HD)),
        in_specs=[spec(SMEM)] + [spec()] * 5,
        out_specs=spec(),
        scratch_shapes=keep + [hold_q],
        compiler_params=params(),
        cost_estimate=pl.CostEstimate(flops=4 * rows * HD * 3072, bytes_accessed=4 << 20, transcendentals=rows * 3072),
        name="attend_far",
    )(place, q_got, every, m, l, a)
    out = lax.all_to_all(result, "seq", 0, 0, tiled=True)

    stored, scales = pl.pallas_call(
        pick_pages,
        out_shape=(shaped((2, PAGE, WIDE)), shaped((2, 2))),
        in_specs=[spec(SMEM), spec(SMEM), spec()],
        out_specs=(spec(), spec()),
        compiler_params=params(),
        name="pick_pages",
    )(place, owners, every)

    attention = pl.pallas_call(
        unpack_out,
        out_shape=shaped((TOK, HQ * HD)),
        in_specs=[spec()],
        out_specs=spec(),
        compiler_params=params(),
        name="unpack_out",
    )(out)
    return attention[None], stored[None, None], scales[None, None]


def solution(mesh):
    sizes = mesh.shape
    devices = mesh.devices.reshape(sizes["seq"], sizes["dec"] // NX, NX, sizes["rep"])
    whole = Mesh(devices, ("seq", "y", "x", "rep"))
    dec = ("y", "x")
    return jax.shard_map(
        on_device,
        mesh=whole,
        in_specs=(
            P(("rep",) + dec, "seq", None),
            P(("rep",) + dec, "seq", None),
            P(("rep",) + dec, "seq"),
            P(("rep", "seq"), None),
            P("rep"),
        ),
        out_specs=(
            P(("rep",) + dec, "seq", None),
            P(("rep", "seq"), dec, None, None, None),
            P(("rep", "seq"), dec, None, None),
        ),
        check_vma=False,
    )
```

```python
import math

import jax
import jax.numpy as jnp
import numpy as np
from jax import lax
from jax.experimental import pallas as pl
from jax.experimental.pallas import tpu as pltpu
from jax.sharding import Mesh, PartitionSpec as P

HQ = 64
KVH = 8
HD = 128
PAGE = 128
GROUP = HQ // KVH
TOK = 16
WIDE = 2 * HD
QW = GROUP * HD
ROWS = GROUP * PAGE
NX = 4
NY = 8
PRE = 32
SLAB = NY * PAGE
KEYS = SLAB + NY * PRE
SLOTS = 2
CHUNK = 512

rope_base = 1000000.0
tiny = 1e-06
masked = -1e30
to_exp2 = HD ** (-0.5) * math.log2(math.e)

VMEM = pltpu.VMEM
SMEM = pltpu.SMEM
f32 = jnp.float32
bf16 = jnp.bfloat16


def spec(space=VMEM):
    return pl.BlockSpec(memory_space=space)


def params(mib=48):
    return pltpu.CompilerParams(vmem_limit_bytes=mib * 1024 * 1024)


def cost(flops, moved, exps=0):
    return pl.CostEstimate(flops=flops, bytes_accessed=moved, transcendentals=exps)


def shaped(shape, dtype=bf16):
    return jax.ShapeDtypeStruct(shape, dtype)


def pack(pos_ref, inv_ref, q_ref, kv_ref, out_ref):
    row = lax.broadcasted_iota(jnp.int32, (TOK, HD), 0) + pos_ref[0]
    angles = row.astype(f32) * inv_ref[...]
    lane = lax.broadcasted_iota(jnp.int32, (TOK, HD), 1)
    cosine = jnp.cos(angles)
    sinus = jnp.sin(angles)
    sinus = jnp.where(lane < HD // 2, -sinus, sinus)

    def turn(x):
        x = x.astype(f32)
        return (x * cosine + pltpu.roll(x, HD // 2, 1) * sinus).astype(bf16)

    for h in range(KVH):
        for g in range(GROUP):
            q = h * GROUP + g
            out_ref[h, :, g * HD : (g + 1) * HD] = turn(q_ref[:, q * HD : (q + 1) * HD])
        out_ref[h, :, QW : QW + HD] = turn(kv_ref[:, h * WIDE : h * WIDE + HD])
        out_ref[h, :, QW + HD :] = kv_ref[:, h * WIDE + HD : (h + 1) * WIDE]


def spread(in_ref, pre_ref, kv_ref, q_ref):
    own = in_ref[:, :, QW:].reshape(PAGE, WIDE)
    pre = pre_ref[...]
    for j in range(NY):
        kv_ref[j, :PAGE] = own
        kv_ref[j, PAGE:] = pre
    for g in range(GROUP):
        q_ref[g * PAGE : (g + 1) * PAGE] = in_ref[:, :, g * HD : (g + 1) * HD].reshape(PAGE, HD)


def offer_pages(place_ref, own_ref, col_ref, out_ref):
    y, x = place_ref[0], place_ref[1]
    pages = own_ref.shape[1]
    lane = lax.broadcasted_iota(jnp.int32, (TOK, WIDE), 1)
    for dest in range(NX):
        me = y * NX + dest

        def look(i, found, me=me):
            one, two = found
            p = pages - 1 - i
            hit = own_ref[0, p] == me
            return jnp.where(hit, p, one), jnp.where(hit, one, two)

        found = lax.fori_loop(0, pages, look, (jnp.int32(pages), jnp.int32(pages)))
        for slot in range(SLOTS):
            page = found[slot]
            here = (page < pages) & (page % NX == x)
            at = slice(slot * PAGE, (slot + 1) * PAGE)
            top_at = slice(SLOTS * PAGE + slot * TOK, SLOTS * PAGE + (slot + 1) * TOK)

            @pl.when(here)
            def _(page=page, dest=dest, at=at, top_at=top_at):
                both = col_ref[page // NX, :PAGE, :].astype(f32)
                tops = []
                for half in range(2):
                    part = both[:, half * HD : (half + 1) * HD]
                    top = jnp.max(jnp.max(jnp.abs(part), axis=0, keepdims=True), axis=1, keepdims=True)
                    out_ref[dest, at, half * HD : (half + 1) * HD] = (part / (top + tiny)).astype(bf16)
                    tops.append(top)
                out_ref[dest, top_at, :] = jnp.where(lane < HD, tops[0], tops[1]).astype(bf16)

            @pl.when(jnp.logical_not(here))
            def _(dest=dest, at=at, top_at=top_at):
                out_ref[dest, at, :] = jnp.zeros((PAGE, WIDE), bf16)
                out_ref[dest, top_at, :] = jnp.zeros((TOK, WIDE), bf16)


def attend(place_ref, col_ref, q0_ref, q1_ref, q2_ref, q3_ref, out_ref, kt_ref, v_ref, s_ref, p_ref, l_ref, h_ref):
    y, x, begin = place_ref[0], place_ref[1], place_ref[2]
    queries = (q0_ref, q1_ref, q2_ref, q3_ref)
    for j in range(NY):
        b = (y + j) % NY
        kt_ref[:, j * PAGE : (j + 1) * PAGE] = col_ref[b, :PAGE, :HD].T
        v_ref[j * PAGE : (j + 1) * PAGE] = col_ref[b, :PAGE, HD:]
    kt_ref[:, SLAB:] = col_ref[:, PAGE:, :HD].reshape(NY * PRE, HD).T
    v_ref[SLAB:] = col_ref[:, PAGE:, HD:].reshape(NY * PRE, HD)

    c = lax.broadcasted_iota(jnp.int32, (1, KEYS), 1)
    b = (y + c // PAGE) % NY
    i = c - SLAB
    slab_bias = jnp.where((c < PAGE) | (b < y), 0.0, masked)
    prefix_bias = jnp.where(((i // PRE) * NX + x) * PRE + i % PRE < begin, 0.0, masked)
    bias = jnp.where(c < SLAB, slab_bias, prefix_bias)
    token = lax.broadcasted_iota(jnp.int32, (CHUNK, PAGE), 0) % PAGE
    own_key = lax.broadcasted_iota(jnp.int32, (CHUNK, PAGE), 1)
    lane = lax.broadcasted_iota(jnp.int32, (PAGE, HD), 1)
    per_set = ROWS // CHUNK
    total = NX * per_set

    def score(t):
        k, part = divmod(t, per_set)
        dest = (x + k) % NX
        reach = jnp.where(dest > x, PAGE, jnp.where(dest == x, 0, -PAGE))
        q = queries[k][part * CHUNK : (part + 1) * CHUNK]
        s = jnp.dot(q, kt_ref[...], preferred_element_type=f32) + bias
        at = slice(t % 2 * CHUNK, (t % 2 + 1) * CHUNK)
        s_ref[at, :PAGE] = jnp.where(own_key <= token + reach, s[:, :PAGE], masked)
        s_ref[at, PAGE:] = s[:, PAGE:]

    def weigh(t):
        at = slice(t % 2 * CHUNK, (t % 2 + 1) * CHUNK)
        s = s_ref[at, :]
        top = s[:, :HD]
        for n in range(1, KEYS // HD):
            top = jnp.maximum(top, s[:, n * HD : (n + 1) * HD])
        high = jnp.max(top, axis=1, keepdims=True) * to_exp2
        p = jnp.exp2(s * to_exp2 - high)
        mass = p[:, :HD]
        for n in range(1, KEYS // HD):
            mass = mass + p[:, n * HD : (n + 1) * HD]
        l_ref[at, :] = mass
        h_ref[at, :] = jnp.broadcast_to(high, (CHUNK, HD))
        p_ref[at, :] = p.astype(bf16)

    def gather(t, stats):
        k, part = divmod(t, per_set)
        dest = (x + k) % NX
        at = slice(t % 2 * CHUNK, (t % 2 + 1) * CHUNK)
        num = jnp.dot(p_ref[at, :], v_ref[...], preferred_element_type=f32)
        mass = jnp.sum(l_ref[at, :], axis=1, keepdims=True)
        out_ref[dest, part * CHUNK : (part + 1) * CHUNK] = (num / mass).astype(bf16)
        level = h_ref[at, :] + jnp.log2(mass)
        for g in range(CHUNK // PAGE):
            one = level[g * PAGE : (g + 1) * PAGE]
            for piece in range(3):
                rounded = one.astype(bf16).astype(f32)
                stats = jnp.where(lane == (part * (CHUNK // PAGE) + g) * 3 + piece, rounded, stats)
                one = one - rounded
        if part == per_set - 1:
            out_ref[dest, ROWS:] = stats.astype(bf16)
        return stats

    stats = None
    for t in range(total + 2):
        if t >= 2:
            if (t - 2) % per_set == 0:
                stats = jnp.zeros((PAGE, HD), f32)
            stats = gather(t - 2, stats)
        if t < total:
            score(t)
        if 1 <= t < total + 1:
            weigh(t - 1)


def combine(in_ref, out_ref):
    stats = [in_ref[i, ROWS:].astype(f32) for i in range(NX)]
    for g in range(GROUP):
        levels = [s[:, 3 * g : 3 * g + 1] + s[:, 3 * g + 1 : 3 * g + 2] + s[:, 3 * g + 2 : 3 * g + 3] for s in stats]
        top = jnp.maximum(jnp.maximum(levels[0], levels[1]), jnp.maximum(levels[2], levels[3]))
        shares = [jnp.exp2(v - top) for v in levels]
        whole = shares[0] + shares[1] + shares[2] + shares[3]
        done = jnp.zeros((PAGE, HD), f32)
        for i in range(NX):
            done = done + in_ref[i, g * PAGE : (g + 1) * PAGE].astype(f32) * (shares[i] / whole)
        out_ref[:, :, g * HD : (g + 1) * HD] = done.astype(bf16).reshape(KVH, TOK, HD)


def unpack(in_ref, out_ref):
    for h in range(KVH):
        out_ref[:, h * QW : (h + 1) * QW] = in_ref[h]


def keep_pages(in_ref, store_ref, scale_ref):
    for slot in range(SLOTS):
        store_ref[slot] = in_ref[slot * PAGE : (slot + 1) * PAGE]
    row = lax.broadcasted_iota(jnp.int32, (2, 2), 0)
    col = lax.broadcasted_iota(jnp.int32, (2, 2), 1)
    first = in_ref[SLOTS * PAGE : SLOTS * PAGE + TOK].astype(f32)
    second = in_ref[SLOTS * PAGE + TOK :].astype(f32)
    upper = jnp.where(col == 0, first[:1, :1], first[:1, HD : HD + 1])
    lower = jnp.where(col == 0, second[:1, :1], second[:1, HD : HD + 1])
    scale_ref[...] = jnp.where(row == 0, upper, lower).astype(bf16)


def on_device(queries, slab_kv, prefix_kv, owners, offset):
    y, x, s = lax.axis_index("y"), lax.axis_index("x"), lax.axis_index("seq")
    begin = offset[0]
    position = (begin + (y * NX + x) * PAGE + s * TOK).reshape(1)
    place = jnp.stack([y, x, begin]).astype(jnp.int32)
    half = np.arange(HD // 2, dtype=np.float64) * 2.0 / HD
    inverse = np.tile((rope_base ** (-half)).astype(np.float32), 2)[None]

    packed = pl.pallas_call(
        pack,
        out_shape=shaped((KVH, TOK, QW + WIDE)),
        in_specs=[spec(SMEM), spec(), spec(), spec()],
        out_specs=spec(),
        compiler_params=params(),
        name="pack",
    )(position, jnp.asarray(inverse), queries[0], slab_kv[0])
    grouped = lax.all_to_all(packed, "seq", 0, 0, tiled=True)

    kv_send, q_own = pl.pallas_call(
        spread,
        out_shape=(shaped((NY, PAGE + PRE, WIDE)), shaped((ROWS, HD))),
        in_specs=[spec(), spec()],
        out_specs=(spec(), spec()),
        compiler_params=params(),
        name="spread",
    )(grouped, prefix_kv)
    column = lax.all_to_all(kv_send, "y", 0, 0, tiled=True)
    asked = [q_own] + [lax.ppermute(q_own, "x", [(i, (i - k) % NX) for i in range(NX)]) for k in range(1, NX)]

    offered = pl.pallas_call(
        offer_pages,
        out_shape=shaped((NX, SLOTS * (PAGE + TOK), WIDE)),
        in_specs=[spec(SMEM), spec(SMEM), spec()],
        out_specs=spec(),
        compiler_params=params(),
        name="offer_pages",
    )(place, owners, column)
    delivered = lax.psum_scatter(
        offered.reshape(NX * SLOTS * (PAGE + TOK), WIDE), "x", scatter_dimension=0, tiled=True
    )

    parts = pl.pallas_call(
        attend,
        out_shape=shaped((NX, ROWS + PAGE, HD)),
        in_specs=[spec(SMEM)] + [spec()] * 5,
        out_specs=spec(),
        scratch_shapes=[
            VMEM((HD, KEYS), bf16),
            VMEM((KEYS, HD), bf16),
            VMEM((2 * CHUNK, KEYS), f32),
            VMEM((2 * CHUNK, KEYS), bf16),
            VMEM((2 * CHUNK, HD), f32),
            VMEM((2 * CHUNK, HD), f32),
        ],
        compiler_params=params(),
        cost_estimate=cost(4 * NX * ROWS * KEYS * HD, 4 << 20, NX * ROWS * KEYS),
        name="attend",
    )(place, column, *asked)
    parts = lax.all_to_all(parts, "x", 0, 0, tiled=True)
    result = pl.pallas_call(
        combine,
        out_shape=shaped((KVH, TOK, QW)),
        in_specs=[spec()],
        out_specs=spec(),
        compiler_params=params(),
        name="combine",
    )(parts)
    back = lax.all_to_all(result, "seq", 0, 0, tiled=True)
    attention = pl.pallas_call(
        unpack,
        out_shape=shaped((TOK, HQ * HD)),
        in_specs=[spec()],
        out_specs=spec(),
        compiler_params=params(),
        name="unpack",
    )(back)
    stored, scales = pl.pallas_call(
        keep_pages,
        out_shape=(shaped((SLOTS, PAGE, WIDE)), shaped((2, 2))),
        in_specs=[spec()],
        out_specs=(spec(), spec()),
        compiler_params=params(),
        name="keep_pages",
    )(delivered)
    return attention[None], stored[None, None], scales[None, None]


def solution(mesh):
    sizes = mesh.shape
    devices = mesh.devices.reshape(sizes["seq"], NY, NX, sizes["rep"])
    whole = Mesh(devices, ("seq", "y", "x", "rep"))
    dec = ("y", "x")
    return jax.shard_map(
        on_device,
        mesh=whole,
        in_specs=(
            P(("rep",) + dec, "seq", None),
            P(("rep",) + dec, "seq", None),
            P(("rep",) + dec, "seq"),
            P(("rep", "seq"), None),
            P("rep"),
        ),
        out_specs=(
            P(("rep",) + dec, "seq", None),
            P(("rep", "seq"), dec, None, None, None),
            P(("rep", "seq"), dec, None, None),
        ),
        check_vma=False,
    )
```

```python
import math

import jax
import jax.numpy as jnp
import numpy as np
from jax import lax
from jax.experimental import pallas as pl
from jax.experimental.pallas import tpu as pltpu
from jax.sharding import Mesh, PartitionSpec as P

HQ = 64
KVH = 8
HD = 128
PAGE = 128
GROUP = HQ // KVH
TOK = 16
WIDE = 2 * HD
QW = GROUP * HD
ROWS = GROUP * PAGE
NX = 4
NY = 8
PRE = 32
SLAB = NY * PAGE
KEYS = SLAB + NY * PRE
SLOTS = 2
CHUNK = 512
TOPS = ROWS + PAGE + SLOTS * 2 * PAGE

rope_base = 1000000.0
tiny = 1e-06
masked = -1e30
to_exp2 = HD ** (-0.5) * math.log2(math.e)

VMEM = pltpu.VMEM
SMEM = pltpu.SMEM
f32 = jnp.float32
bf16 = jnp.bfloat16


def spec(space=VMEM):
    return pl.BlockSpec(memory_space=space)


def params(mib=48):
    return pltpu.CompilerParams(vmem_limit_bytes=mib * 1024 * 1024)


def cost(flops, moved, exps=0):
    return pl.CostEstimate(flops=flops, bytes_accessed=moved, transcendentals=exps)


def shaped(shape, dtype=bf16):
    return jax.ShapeDtypeStruct(shape, dtype)


def pack(pos_ref, q_hbm, kv_hbm, out_ref, q_ref, kv_ref, sems):
    fetch_q = pltpu.make_async_copy(q_hbm, q_ref, sems.at[0])
    fetch_kv = pltpu.make_async_copy(kv_hbm, kv_ref, sems.at[1])
    fetch_q.start()
    fetch_kv.start()
    half = HD // 2
    lane = lax.broadcasted_iota(jnp.int32, (TOK, HD), 1)
    place = lane % half
    inverse = jnp.zeros((TOK, HD), f32)
    for k in range(half):
        inverse = jnp.where(place == k, float(np.float32(rope_base ** (-2.0 * k / HD))), inverse)
    row = lax.broadcasted_iota(jnp.int32, (TOK, HD), 0) + pos_ref[0]
    angles = row.astype(f32) * inverse
    cosine = jnp.cos(angles)
    sinus = jnp.sin(angles)
    sinus = jnp.where(lane < half, -sinus, sinus)

    def turn(x):
        x = x.astype(f32)
        return (x * cosine + pltpu.roll(x, half, 1) * sinus).astype(bf16)

    fetch_kv.wait()
    for h in range(KVH):
        out_ref[h, :, QW : QW + HD] = turn(kv_ref[:, h * WIDE : h * WIDE + HD])
        out_ref[h, :, QW + HD :] = kv_ref[:, h * WIDE + HD : (h + 1) * WIDE]
    fetch_q.wait()
    for h in range(KVH):
        for g in range(GROUP):
            q = h * GROUP + g
            out_ref[h, :, g * HD : (g + 1) * HD] = turn(q_ref[:, q * HD : (q + 1) * HD])


def spread(in_ref, pre_ref, kv_ref, q_ref):
    own = in_ref[:, :, QW:].reshape(PAGE, WIDE)
    pre = pre_ref[...]
    for j in range(NY):
        kv_ref[j, :PAGE] = own
        kv_ref[j, PAGE:] = pre
    for g in range(GROUP):
        q_ref[g * PAGE : (g + 1) * PAGE] = in_ref[:, :, g * HD : (g + 1) * HD].reshape(PAGE, HD)


def offer_pages(x, y, own_ref, col_ref, out_ref):
    pages = own_ref.shape[1]
    found = [[jnp.int32(pages)] * SLOTS for _ in range(NX)]
    for p in reversed(range(pages)):
        dest = own_ref[0, p] - y * NX
        for d in range(NX):
            one, two = found[d]
            found[d] = [jnp.where(dest == d, p, one), jnp.where(dest == d, one, two)]
    tops = []
    for d in range(NX):
        tops.append([])
        for slot in range(SLOTS):
            page = found[d][slot]
            held = jnp.where((page < pages) & (page % NX == x), 1.0, 0.0)
            row = jnp.minimum(page // NX, NY - 1)
            for half in range(2):
                part = col_ref[row, :PAGE, half * HD : (half + 1) * HD].astype(f32)
                top = jnp.max(jnp.max(jnp.abs(part), axis=0, keepdims=True), axis=1, keepdims=True)
                at = ROWS + PAGE + (slot * 2 + half) * PAGE
                out_ref[d, at : at + PAGE] = (part * (held / (top + tiny))).astype(bf16)
                tops[d].append(top * held)
    return tops


def attend(place_ref, own_ref, col_ref, q0_ref, q1_ref, q2_ref, q3_ref, out_ref, kt_ref, v_ref, s_ref, p_ref, l_ref, h_ref):
    y, x, begin = place_ref[0], place_ref[1], place_ref[2]
    queries = (q0_ref, q1_ref, q2_ref, q3_ref)
    for j in range(NY):
        b = (y + j) % NY
        kt_ref[:, j * PAGE : (j + 1) * PAGE] = col_ref[b, :PAGE, :HD].T
        v_ref[j * PAGE : (j + 1) * PAGE] = col_ref[b, :PAGE, HD:]
    kt_ref[:, SLAB:] = col_ref[:, PAGE:, :HD].reshape(NY * PRE, HD).T
    v_ref[SLAB:] = col_ref[:, PAGE:, HD:].reshape(NY * PRE, HD)

    c = lax.broadcasted_iota(jnp.int32, (1, KEYS), 1)
    b = (y + c // PAGE) % NY
    i = c - SLAB
    slab_bias = jnp.where((c < PAGE) | (b < y), 0.0, masked)
    prefix_bias = jnp.where(((i // PRE) * NX + x) * PRE + i % PRE < begin, 0.0, masked)
    bias = jnp.where(c < SLAB, slab_bias, prefix_bias)
    token = lax.broadcasted_iota(jnp.int32, (CHUNK, PAGE), 0) % PAGE
    own_key = lax.broadcasted_iota(jnp.int32, (CHUNK, PAGE), 1)
    lane = lax.broadcasted_iota(jnp.int32, (PAGE, HD), 1)
    per_set = ROWS // CHUNK
    total = NX * per_set

    def score(t):
        k, part = divmod(t, per_set)
        dest = (x + k) % NX
        reach = jnp.where(dest > x, PAGE, jnp.where(dest == x, 0, -PAGE))
        q = queries[k][part * CHUNK : (part + 1) * CHUNK]
        s = jnp.dot(q, kt_ref[...], preferred_element_type=f32) + bias
        at = slice(t % 2 * CHUNK, (t % 2 + 1) * CHUNK)
        s_ref[at, :PAGE] = jnp.where(own_key <= token + reach, s[:, :PAGE], masked)
        s_ref[at, PAGE:] = s[:, PAGE:]

    def weigh(t):
        at = slice(t % 2 * CHUNK, (t % 2 + 1) * CHUNK)
        s = s_ref[at, :]
        top = s[:, :HD]
        for n in range(1, KEYS // HD):
            top = jnp.maximum(top, s[:, n * HD : (n + 1) * HD])
        high = jnp.max(top, axis=1, keepdims=True) * to_exp2
        p = jnp.exp2(s * to_exp2 - high)
        mass = p[:, :HD]
        for n in range(1, KEYS // HD):
            mass = mass + p[:, n * HD : (n + 1) * HD]
        l_ref[at, :] = mass
        h_ref[at, :] = jnp.broadcast_to(high, (CHUNK, HD))
        p_ref[at, :] = p.astype(bf16)

    def gather(t, stats):
        k, part = divmod(t, per_set)
        dest = (x + k) % NX
        at = slice(t % 2 * CHUNK, (t % 2 + 1) * CHUNK)
        num = jnp.dot(p_ref[at, :], v_ref[...], preferred_element_type=f32)
        mass = jnp.sum(l_ref[at, :], axis=1, keepdims=True)
        out_ref[dest, part * CHUNK : (part + 1) * CHUNK] = (num / mass).astype(bf16)
        level = h_ref[at, :] + jnp.log2(mass)
        for g in range(CHUNK // PAGE):
            one = level[g * PAGE : (g + 1) * PAGE]
            for piece in range(3):
                rounded = one.astype(bf16).astype(f32)
                stats = jnp.where(lane == (part * (CHUNK // PAGE) + g) * 3 + piece, rounded, stats)
                one = one - rounded
        if part == per_set - 1:
            out_ref[dest, ROWS : ROWS + PAGE] = stats.astype(bf16)
        return stats

    tops = offer_pages(x, y, own_ref, col_ref, out_ref)
    stats = None
    for t in range(total + 2):
        if t >= 2:
            if (t - 2) % per_set == 0:
                stats = jnp.zeros((PAGE, HD), f32)
            stats = gather(t - 2, stats)
        if t < total:
            score(t)
        if 1 <= t < total + 1:
            weigh(t - 1)
    narrow = lax.broadcasted_iota(jnp.int32, (TOK, HD), 1)
    for d in range(NX):
        rows = jnp.zeros((TOK, HD), f32)
        for n, top in enumerate(tops[d]):
            rows = jnp.where(narrow == n, top, rows)
        out_ref[d, TOPS:] = rows.astype(bf16)


def combine(in_ref, out_ref):
    stats = [in_ref[i, ROWS : ROWS + PAGE].astype(f32) for i in range(NX)]
    for g in range(GROUP):
        levels = [s[:, 3 * g : 3 * g + 1] + s[:, 3 * g + 1 : 3 * g + 2] + s[:, 3 * g + 2 : 3 * g + 3] for s in stats]
        top = jnp.maximum(jnp.maximum(levels[0], levels[1]), jnp.maximum(levels[2], levels[3]))
        shares = [jnp.exp2(v - top) for v in levels]
        whole = shares[0] + shares[1] + shares[2] + shares[3]
        done = jnp.zeros((PAGE, HD), f32)
        for i in range(NX):
            done = done + in_ref[i, g * PAGE : (g + 1) * PAGE].astype(f32) * (shares[i] / whole)
        out_ref[:, :, g * HD : (g + 1) * HD] = done.astype(bf16).reshape(KVH, TOK, HD)


def unpack(in_ref, out_ref):
    for h in range(KVH):
        out_ref[:, h * QW : (h + 1) * QW] = in_ref[h]


def keep_pages(in_ref, store_ref, scale_ref):
    for slot in range(SLOTS):
        for half in range(2):
            at = ROWS + PAGE + (slot * 2 + half) * PAGE
            part = in_ref[0, at : at + PAGE].astype(f32)
            for i in range(1, NX):
                part = part + in_ref[i, at : at + PAGE].astype(f32)
            store_ref[slot, :, half * HD : (half + 1) * HD] = part.astype(bf16)
    tops = in_ref[0, TOPS:].astype(f32)
    for i in range(1, NX):
        tops = tops + in_ref[i, TOPS:].astype(f32)
    row = lax.broadcasted_iota(jnp.int32, (2, 2), 0)
    col = lax.broadcasted_iota(jnp.int32, (2, 2), 1)
    upper = jnp.where(col == 0, tops[:1, 0:1], tops[:1, 1:2])
    lower = jnp.where(col == 0, tops[:1, 2:3], tops[:1, 3:4])
    scale_ref[...] = jnp.where(row == 0, upper, lower).astype(bf16)


def on_device(queries, slab_kv, prefix_kv, owners, offset):
    y, x, s = lax.axis_index("y"), lax.axis_index("x"), lax.axis_index("seq")
    begin = offset[0]
    position = (begin + (y * NX + x) * PAGE + s * TOK).reshape(1)
    place = jnp.stack([y, x, begin]).astype(jnp.int32)

    packed = pl.pallas_call(
        pack,
        out_shape=shaped((KVH, TOK, QW + WIDE)),
        in_specs=[spec(SMEM), spec(pltpu.HBM), spec(pltpu.HBM)],
        out_specs=spec(),
        scratch_shapes=[VMEM((TOK, HQ * HD), bf16), VMEM((TOK, KVH * WIDE), bf16), pltpu.SemaphoreType.DMA((2,))],
        compiler_params=params(60),
        name="pack",
    )(position, queries[0], slab_kv[0])
    grouped = lax.all_to_all(packed, "seq", 0, 0, tiled=True)

    kv_send, q_own = pl.pallas_call(
        spread,
        out_shape=(shaped((NY, PAGE + PRE, WIDE)), shaped((ROWS, HD))),
        in_specs=[spec(), spec()],
        out_specs=(spec(), spec()),
        compiler_params=params(),
        name="spread",
    )(grouped, prefix_kv)
    column = lax.all_to_all(kv_send, "y", 0, 0, tiled=True)
    asked = [q_own] + [lax.ppermute(q_own, "x", [(i, (i - k) % NX) for i in range(NX)]) for k in range(1, NX)]

    parts = pl.pallas_call(
        attend,
        out_shape=shaped((NX, TOPS + TOK, HD)),
        in_specs=[spec(SMEM), spec(SMEM)] + [spec()] * 5,
        out_specs=spec(),
        scratch_shapes=[
            VMEM((HD, KEYS), bf16),
            VMEM((KEYS, HD), bf16),
            VMEM((2 * CHUNK, KEYS), f32),
            VMEM((2 * CHUNK, KEYS), bf16),
            VMEM((2 * CHUNK, HD), f32),
            VMEM((2 * CHUNK, HD), f32),
        ],
        compiler_params=params(),
        cost_estimate=cost(4 * NX * ROWS * KEYS * HD, 4 << 20, NX * ROWS * KEYS),
        name="attend",
    )(place, owners, column, *asked)
    parts = lax.all_to_all(parts, "x", 0, 0, tiled=True)
    result = pl.pallas_call(
        combine,
        out_shape=shaped((KVH, TOK, QW)),
        in_specs=[spec()],
        out_specs=spec(),
        compiler_params=params(),
        name="combine",
    )(parts)
    back = lax.all_to_all(result, "seq", 0, 0, tiled=True)
    attention = pl.pallas_call(
        unpack,
        out_shape=shaped((TOK, HQ * HD)),
        in_specs=[spec()],
        out_specs=spec(),
        compiler_params=params(),
        name="unpack",
    )(back)
    stored, scales = pl.pallas_call(
        keep_pages,
        out_shape=(shaped((SLOTS, PAGE, WIDE)), shaped((2, 2))),
        in_specs=[spec()],
        out_specs=(spec(), spec()),
        compiler_params=params(),
        name="keep_pages",
    )(parts)
    return attention[None], stored[None, None], scales[None, None]


def solution(mesh):
    sizes = mesh.shape
    devices = mesh.devices.reshape(sizes["seq"], NY, NX, sizes["rep"])
    whole = Mesh(devices, ("seq", "y", "x", "rep"))
    dec = ("y", "x")
    return jax.shard_map(
        on_device,
        mesh=whole,
        in_specs=(
            P(("rep",) + dec, "seq", None),
            P(("rep",) + dec, "seq", None),
            P(("rep",) + dec, "seq"),
            P(("rep", "seq"), None),
            P("rep"),
        ),
        out_specs=(
            P(("rep",) + dec, "seq", None),
            P(("rep", "seq"), dec, None, None, None),
            P(("rep", "seq"), dec, None, None),
        ),
        check_vma=False,
    )
```

```python
import math

import jax
import jax.numpy as jnp
import numpy as np
from jax import lax
from jax.experimental import pallas as pl
from jax.experimental.pallas import tpu as pltpu
from jax.sharding import Mesh, PartitionSpec as P

HQ = 64
KVH = 8
HD = 128
PAGE = 128
GROUP = HQ // KVH
TOK = 16
WIDE = 2 * HD
QW = GROUP * HD
ROWS = GROUP * PAGE
NX = 4
NY = 8
PRE = 32
SLAB = NY * PAGE
KEYS = SLAB + NY * PRE
SLOTS = 2
CHUNK = 512
MESSAGE = (GROUP + 1) * TOK

rope_base = 1000000.0
tiny = 1e-06
masked = -1e30
to_exp2 = HD ** (-0.5) * math.log2(math.e)

VMEM = pltpu.VMEM
SMEM = pltpu.SMEM
f32 = jnp.float32
bf16 = jnp.bfloat16


def spec(space=VMEM):
    return pl.BlockSpec(memory_space=space)


def params(mib=32):
    return pltpu.CompilerParams(vmem_limit_bytes=mib * 1024 * 1024)


def cost(flops, moved, exps=0):
    return pl.CostEstimate(flops=flops, bytes_accessed=moved, transcendentals=exps)


def shaped(shape, dtype=bf16):
    return jax.ShapeDtypeStruct(shape, dtype)


def pack(offset_ref, q_hbm, kv_hbm, out_ref, q_ref, kv_ref, sems):
    block = lax.axis_index("y") * NX + lax.axis_index("x")
    first = offset_ref[0] + block * PAGE + lax.axis_index("seq") * TOK
    fetch_q = pltpu.make_async_copy(q_hbm, q_ref, sems.at[0])
    fetch_kv = pltpu.make_async_copy(kv_hbm, kv_ref, sems.at[1])
    fetch_q.start()
    fetch_kv.start()
    half = HD // 2
    lane = lax.broadcasted_iota(jnp.int32, (TOK, HD), 1)
    place = lane % half
    inverse = jnp.zeros((TOK, HD), f32)
    for k in range(half):
        inverse = jnp.where(place == k, float(np.float32(rope_base ** (-2.0 * k / HD))), inverse)
    row = lax.broadcasted_iota(jnp.int32, (TOK, HD), 0) + first
    angles = row.astype(f32) * inverse
    cosine = jnp.cos(angles)
    sinus = jnp.sin(angles)
    sinus = jnp.where(lane < half, -sinus, sinus)

    def turn(x):
        x = x.astype(f32)
        return (x * cosine + pltpu.roll(x, half, 1) * sinus).astype(bf16)

    fetch_kv.wait()
    for h in range(KVH):
        out_ref[h, :, QW : QW + HD] = turn(kv_ref[:, h * WIDE : h * WIDE + HD])
        out_ref[h, :, QW + HD :] = kv_ref[:, h * WIDE + HD : (h + 1) * WIDE]
    fetch_q.wait()
    for h in range(KVH):
        for g in range(GROUP):
            q = h * GROUP + g
            out_ref[h, :, g * HD : (g + 1) * HD] = turn(q_ref[:, q * HD : (q + 1) * HD])


def spread(in_ref, pre_ref, kv_ref, q_ref):
    own = in_ref[:, :, QW:].reshape(PAGE, WIDE)
    pre = pre_ref[...]
    for j in range(NY):
        kv_ref[j, :PAGE] = own
        kv_ref[j, PAGE:] = pre
    for g in range(GROUP):
        q_ref[g * PAGE : (g + 1) * PAGE] = in_ref[:, :, g * HD : (g + 1) * HD].reshape(PAGE, HD)


def offer_pages(place_ref, own_ref, col_ref, *outs):
    y, x = place_ref[0], place_ref[1]
    pages = own_ref.shape[1]
    found = [[jnp.int32(pages)] * SLOTS for _ in range(NX)]
    owners = [y * NX + (x + k) % NX for k in range(NX)]
    for p in reversed(range(pages)):
        for k in range(NX):
            hit = own_ref[0, p] == owners[k]
            one, two = found[k]
            found[k] = [jnp.where(hit, p, one), jnp.where(hit, one, two)]
    lane = lax.broadcasted_iota(jnp.int32, (TOK, WIDE), 1)
    for k in range(NX):
        tops = jnp.zeros((TOK, WIDE), f32)
        for slot in range(SLOTS):
            page = found[k][slot]
            held = jnp.where((page < pages) & (page % NX == x), 1.0, 0.0)
            row = jnp.minimum(page // NX, NY - 1)
            for half in range(2):
                part = col_ref[row, :PAGE, half * HD : (half + 1) * HD].astype(f32)
                top = jnp.max(jnp.max(jnp.abs(part), axis=0, keepdims=True), axis=1, keepdims=True)
                scaled = part * (held / (top + tiny))
                outs[k][slot * PAGE : (slot + 1) * PAGE, half * HD : (half + 1) * HD] = scaled.astype(bf16)
                tops = jnp.where(lane == slot * 2 + half, top * held, tops)
        outs[k][SLOTS * PAGE :] = tops.astype(bf16)


def attend(place_ref, col_ref, *refs):
    *queries, out_ref, kt_ref, v_ref, s_ref, p_ref, l_ref, h_ref = refs
    y, x, begin = place_ref[0], place_ref[1], place_ref[2]
    for j in range(NY):
        b = (y + j) % NY
        kt_ref[:, j * PAGE : (j + 1) * PAGE] = col_ref[b, :PAGE, :HD].T
        v_ref[j * PAGE : (j + 1) * PAGE] = col_ref[b, :PAGE, HD:]
    kt_ref[:, SLAB:] = col_ref[:, PAGE:, :HD].reshape(NY * PRE, HD).T
    v_ref[SLAB:] = col_ref[:, PAGE:, HD:].reshape(NY * PRE, HD)

    c = lax.broadcasted_iota(jnp.int32, (1, KEYS), 1)
    b = (y + c // PAGE) % NY
    i = c - SLAB
    slab_bias = jnp.where(c < PAGE, 0.0, jnp.where(b < y, 0.0, masked))
    prefix_bias = jnp.where(((i // PRE) * NX + x) * PRE + i % PRE < begin, 0.0, masked)
    bias = jnp.where(c < SLAB, slab_bias, prefix_bias)
    token = lax.broadcasted_iota(jnp.int32, (CHUNK, PAGE), 0) % PAGE
    own_key = lax.broadcasted_iota(jnp.int32, (CHUNK, PAGE), 1)
    lane = lax.broadcasted_iota(jnp.int32, (PAGE, HD), 1)
    per_set = ROWS // CHUNK
    total = NX * per_set

    def score(t):
        n, part = divmod(t, per_set)
        q = queries[n][part * CHUNK : (part + 1) * CHUNK]
        s = jnp.dot(q, kt_ref[...], preferred_element_type=f32) + bias
        at = slice(t % 2 * CHUNK, (t % 2 + 1) * CHUNK)
        if n == 0:
            s_ref[at, :PAGE] = jnp.where(own_key <= token, s[:, :PAGE], masked)
        else:
            s_ref[at, :PAGE] = s[:, :PAGE] + jnp.where((x + n) % NX > x, 0.0, masked)
        s_ref[at, PAGE:] = s[:, PAGE:]

    def weigh(t):
        at = slice(t % 2 * CHUNK, (t % 2 + 1) * CHUNK)
        s = s_ref[at, :]
        top = s[:, :HD]
        for n in range(1, KEYS // HD):
            top = jnp.maximum(top, s[:, n * HD : (n + 1) * HD])
        high = jnp.max(top, axis=1, keepdims=True) * to_exp2
        p = jnp.exp2(s * to_exp2 - high)
        mass = p[:, :HD]
        for n in range(1, KEYS // HD):
            mass = mass + p[:, n * HD : (n + 1) * HD]
        l_ref[at, :] = mass
        h_ref[at, :] = jnp.broadcast_to(high, (CHUNK, HD))
        p_ref[at, :] = p.astype(bf16)

    def gather(t, stats):
        n, part = divmod(t, per_set)

        def put(g, value):
            out_ref[:, (x + n) % NX, g * TOK : (g + 1) * TOK] = value.reshape(KVH, TOK, HD)

        at = slice(t % 2 * CHUNK, (t % 2 + 1) * CHUNK)
        num = jnp.dot(p_ref[at, :], v_ref[...], preferred_element_type=f32)
        mass = jnp.sum(l_ref[at, :], axis=1, keepdims=True)
        done = (num / mass).astype(bf16)
        level = h_ref[at, :] + jnp.log2(mass)
        for m in range(CHUNK // PAGE):
            g = part * (CHUNK // PAGE) + m
            rows = slice(m * PAGE, (m + 1) * PAGE)
            put(g, done[rows])
            one = level[rows]
            for piece in range(3):
                rounded = one.astype(bf16).astype(f32)
                stats = jnp.where(lane == piece * GROUP + g, rounded, stats)
                one = one - rounded
        if part == per_set - 1:
            put(GROUP, stats.astype(bf16))
        return stats

    stats = None
    for t in range(total + 2):
        if t >= 2:
            if (t - 2) % per_set == 0:
                stats = jnp.zeros((PAGE, HD), f32)
            stats = gather(t - 2, stats)
        if t < total:
            score(t)
        if 1 <= t < total + 1:
            weigh(t - 1)


def combine(in_ref, out_ref):
    for h in range(KVH):
        levels = []
        for i in range(NX):
            pieces = in_ref[h * NX + i, GROUP * TOK :].astype(f32)
            levels.append(pieces + pltpu.roll(pieces, HD - GROUP, 1) + pltpu.roll(pieces, HD - 2 * GROUP, 1))
        top = jnp.maximum(jnp.maximum(levels[0], levels[1]), jnp.maximum(levels[2], levels[3]))
        shares = [jnp.exp2(v - top) for v in levels]
        whole = shares[0] + shares[1] + shares[2] + shares[3]
        shares = [v / whole for v in shares]
        for g in range(GROUP):
            done = jnp.zeros((TOK, HD), f32)
            for i in range(NX):
                part = in_ref[h * NX + i, g * TOK : (g + 1) * TOK].astype(f32)
                done = done + part * shares[i][:, g : g + 1]
            out_ref[:, h * QW + g * HD : h * QW + (g + 1) * HD] = done.astype(bf16)


def keep_pages(*refs):
    *ins, store_ref, scale_ref = refs

    def total(at):
        part = ins[0][at].astype(f32)
        for ref in ins[1:]:
            part = part + ref[at].astype(f32)
        return part

    for slot in range(SLOTS):
        store_ref[slot] = total(slice(slot * PAGE, (slot + 1) * PAGE)).astype(bf16)
    tops = total(slice(SLOTS * PAGE, SLOTS * PAGE + TOK))
    row = lax.broadcasted_iota(jnp.int32, (2, 2), 0)
    col = lax.broadcasted_iota(jnp.int32, (2, 2), 1)
    upper = jnp.where(col == 0, tops[:1, 0:1], tops[:1, 1:2])
    lower = jnp.where(col == 0, tops[:1, 2:3], tops[:1, 3:4])
    scale_ref[...] = jnp.where(row == 0, upper, lower).astype(bf16)


def on_device(queries, slab_kv, prefix_kv, owners, offset):
    y, x = lax.axis_index("y"), lax.axis_index("x")
    begin = offset[0]
    place = jnp.stack([y, x, begin]).astype(jnp.int32)

    packed = pl.pallas_call(
        pack,
        out_shape=shaped((KVH, TOK, QW + WIDE)),
        in_specs=[spec(SMEM), spec(pltpu.HBM), spec(pltpu.HBM)],
        out_specs=spec(),
        scratch_shapes=[VMEM((TOK, HQ * HD), bf16), VMEM((TOK, KVH * WIDE), bf16), pltpu.SemaphoreType.DMA((2,))],
        compiler_params=params(60),
        name="pack",
    )(offset, queries[0], slab_kv[0])
    grouped = lax.all_to_all(packed, "seq", 0, 0, tiled=True)

    kv_send, q_own = pl.pallas_call(
        spread,
        out_shape=(shaped((NY, PAGE + PRE, WIDE)), shaped((ROWS, HD))),
        in_specs=[spec(), spec()],
        out_specs=(spec(), spec()),
        compiler_params=params(),
        name="spread",
    )(grouped, prefix_kv)
    column = lax.all_to_all(kv_send, "y", 0, 0, tiled=True)
    asked = [q_own] + [lax.ppermute(q_own, "x", [(i, (i - k) % NX) for i in range(NX)]) for k in range(1, NX)]

    parts = pl.pallas_call(
        attend,
        out_shape=shaped((KVH, NX, MESSAGE, HD)),
        in_specs=[spec(SMEM)] + [spec()] * (1 + NX),
        out_specs=spec(),
        scratch_shapes=[
            VMEM((HD, KEYS), bf16),
            VMEM((KEYS, HD), bf16),
            VMEM((2 * CHUNK, KEYS), f32),
            VMEM((2 * CHUNK, KEYS), bf16),
            VMEM((2 * CHUNK, HD), f32),
            VMEM((2 * CHUNK, HD), f32),
        ],
        compiler_params=params(),
        cost_estimate=cost(4 * NX * ROWS * KEYS * HD, 4 << 20, NX * ROWS * KEYS),
        name="attend",
    )(place, column, *asked)
    parts = lax.all_to_all(parts.reshape(KVH * NX, MESSAGE, HD), ("seq", "x"), 0, 0, tiled=True)

    offered = pl.pallas_call(
        offer_pages,
        out_shape=(shaped((SLOTS * PAGE + TOK, WIDE)),) * NX,
        in_specs=[spec(SMEM), spec(SMEM), spec()],
        out_specs=(spec(),) * NX,
        compiler_params=params(),
        name="offer_pages",
    )(place, owners, column)
    delivered = [offered[0]] + [
        lax.ppermute(offered[k], "x", [(i, (i + k) % NX) for i in range(NX)]) for k in range(1, NX)
    ]
    stored, scales = pl.pallas_call(
        keep_pages,
        out_shape=(shaped((SLOTS, PAGE, WIDE)), shaped((2, 2))),
        in_specs=[spec()] * NX,
        out_specs=(spec(), spec()),
        compiler_params=params(),
        name="keep_pages",
    )(*delivered)
    attention = pl.pallas_call(
        combine,
        out_shape=shaped((TOK, HQ * HD)),
        in_specs=[spec()],
        out_specs=spec(),
        compiler_params=params(),
        name="combine",
    )(parts)
    return attention[None], stored[None, None], scales[None, None]


def solution(mesh):
    sizes = mesh.shape
    devices = mesh.devices.reshape(sizes["seq"], NY, NX, sizes["rep"])
    whole = Mesh(devices, ("seq", "y", "x", "rep"))
    dec = ("y", "x")
    return jax.shard_map(
        on_device,
        mesh=whole,
        in_specs=(
            P(("rep",) + dec, "seq", None),
            P(("rep",) + dec, "seq", None),
            P(("rep",) + dec, "seq"),
            P(("rep", "seq"), None),
            P("rep"),
        ),
        out_specs=(
            P(("rep",) + dec, "seq", None),
            P(("rep", "seq"), dec, None, None, None),
            P(("rep", "seq"), dec, None, None),
        ),
        check_vma=False,
    )
```

```python
import math

import jax
import jax.numpy as jnp
import numpy as np
from jax import lax
from jax.experimental import pallas as pl
from jax.experimental.pallas import tpu as pltpu
from jax.sharding import Mesh, PartitionSpec as P

HQ = 64
KVH = 8
HD = 128
PAGE = 128
GROUP = HQ // KVH
TOK = 16
WIDE = 2 * HD
QW = GROUP * HD
ROWS = GROUP * PAGE
NX = 4
NY = 8
PRE = 32
SLAB = NY * PAGE
KEYS = SLAB + NY * PRE
SLOTS = 2
CHUNK = 512
MESSAGE = (GROUP + 1) * TOK

rope_base = 1000000.0
tiny = 1e-06
masked = -1e30
to_exp2 = HD ** (-0.5) * math.log2(math.e)

VMEM = pltpu.VMEM
SMEM = pltpu.SMEM
f32 = jnp.float32
bf16 = jnp.bfloat16


def spec(space=VMEM):
    return pl.BlockSpec(memory_space=space)


def params(mib=32):
    return pltpu.CompilerParams(vmem_limit_bytes=mib * 1024 * 1024)


def cost(flops, moved, exps=0):
    return pl.CostEstimate(flops=flops, bytes_accessed=moved, transcendentals=exps)


def shaped(shape, dtype=bf16):
    return jax.ShapeDtypeStruct(shape, dtype)


def pack(offset_ref, q_hbm, kv_hbm, out_ref, q_ref, kv_ref, sems):
    block = lax.axis_index("y") * NX + lax.axis_index("x")
    first = offset_ref[0] + block * PAGE + lax.axis_index("seq") * TOK
    fetch_q = pltpu.make_async_copy(q_hbm, q_ref, sems.at[0])
    fetch_kv = pltpu.make_async_copy(kv_hbm, kv_ref, sems.at[1])
    fetch_q.start()
    fetch_kv.start()
    half = HD // 2
    lane = lax.broadcasted_iota(jnp.int32, (TOK, HD), 1)
    place = lane % half
    inverse = jnp.zeros((TOK, HD), f32)
    for k in range(half):
        inverse = jnp.where(place == k, float(np.float32(rope_base ** (-2.0 * k / HD))), inverse)
    row = lax.broadcasted_iota(jnp.int32, (TOK, HD), 0) + first
    angles = row.astype(f32) * inverse
    cosine = jnp.cos(angles)
    sinus = jnp.sin(angles)
    sinus = jnp.where(lane < half, -sinus, sinus)

    def turn(x):
        x = x.astype(f32)
        return (x * cosine + pltpu.roll(x, half, 1) * sinus).astype(bf16)

    fetch_kv.wait()
    for h in range(KVH):
        out_ref[h, :, QW : QW + HD] = turn(kv_ref[:, h * WIDE : h * WIDE + HD])
        out_ref[h, :, QW + HD :] = kv_ref[:, h * WIDE + HD : (h + 1) * WIDE]
    fetch_q.wait()
    for h in range(KVH):
        for g in range(GROUP):
            q = h * GROUP + g
            out_ref[h, :, g * HD : (g + 1) * HD] = turn(q_ref[:, q * HD : (q + 1) * HD])


def spread(in_ref, pre_ref, kv_ref, q_ref):
    own = in_ref[:, :, QW:].reshape(PAGE, WIDE)
    pre = pre_ref[...]
    for j in range(NY):
        kv_ref[j, :PAGE] = own
        kv_ref[j, PAGE:] = pre
    for g in range(GROUP):
        q_ref[g * PAGE : (g + 1) * PAGE] = in_ref[:, :, g * HD : (g + 1) * HD].reshape(PAGE, HD)


def offer_pages(place_ref, own_ref, col_ref, *outs):
    y, x = place_ref[0], place_ref[1]
    pages = own_ref.shape[1]
    found = [[jnp.int32(pages)] * SLOTS for _ in range(NX)]
    owners = [y * NX + (x + k) % NX for k in range(NX)]
    for p in reversed(range(pages)):
        for k in range(NX):
            hit = own_ref[0, p] == owners[k]
            one, two = found[k]
            found[k] = [jnp.where(hit, p, one), jnp.where(hit, one, two)]
    lane = lax.broadcasted_iota(jnp.int32, (TOK, WIDE), 1)
    for k in range(NX):
        tops = jnp.zeros((TOK, WIDE), f32)
        for slot in range(SLOTS):
            page = found[k][slot]
            held = jnp.where((page < pages) & (page % NX == x), 1.0, 0.0)
            row = jnp.minimum(page // NX, NY - 1)
            for half in range(2):
                part = col_ref[row, :PAGE, half * HD : (half + 1) * HD].astype(f32)
                top = jnp.max(jnp.max(jnp.abs(part), axis=0, keepdims=True), axis=1, keepdims=True)
                scaled = part * (held / (top + tiny))
                outs[k][slot * PAGE : (slot + 1) * PAGE, half * HD : (half + 1) * HD] = scaled.astype(bf16)
                tops = jnp.where(lane == slot * 2 + half, top * held, tops)
        outs[k][SLOTS * PAGE :] = tops.astype(bf16)


def attend(place_ref, col_ref, *refs):
    *queries, out_hbm, k_ref, v_ref, s_ref, p_ref, l_ref, h_ref, out_ref, sems = refs
    y, x, begin = place_ref[0], place_ref[1], place_ref[2]
    for at, j in [(0, 0)] + [(PAGE + NY * PRE + (j - 1) * PAGE, j) for j in range(1, NY)]:
        b = (y - j + NY) % NY
        k_ref[at : at + PAGE] = col_ref[b, :PAGE, :HD]
        v_ref[at : at + PAGE] = col_ref[b, :PAGE, HD:]
    shared = slice(PAGE, PAGE + NY * PRE)
    k_ref[shared] = col_ref[:, PAGE:, :HD].reshape(NY * PRE, HD)
    v_ref[shared] = col_ref[:, PAGE:, HD:].reshape(NY * PRE, HD)

    i = lax.broadcasted_iota(jnp.int32, (1, NY * PRE), 1)
    prefix_bias = jnp.where(((i // PRE) * NX + x) * PRE + i % PRE < begin, 0.0, masked)
    token = lax.broadcasted_iota(jnp.int32, (CHUNK, PAGE), 0) % PAGE
    own_key = lax.broadcasted_iota(jnp.int32, (CHUNK, PAGE), 1)
    lane = lax.broadcasted_iota(jnp.int32, (PAGE, HD), 1)
    per_set = ROWS // CHUNK
    total = NX * per_set

    def run(blocks):
        keys = PAGE + NY * PRE + blocks * PAGE
        last_bias = jnp.where(y >= blocks, 0.0, masked)

        def score(t):
            n, part = divmod(t, per_set)
            q = queries[n][part * CHUNK : (part + 1) * CHUNK]
            s = lax.dot_general(q, k_ref[:keys], (((1,), (1,)), ((), ())), preferred_element_type=f32)
            at = slice(t % 2 * CHUNK, (t % 2 + 1) * CHUNK)
            if n == 0:
                s_ref[at, :PAGE] = jnp.where(own_key <= token, s[:, :PAGE], masked)
            else:
                s_ref[at, :PAGE] = s[:, :PAGE] + jnp.where((x + n) % NX > x, 0.0, masked)
            s_ref[at, shared] = s[:, shared] + prefix_bias
            if blocks > 1:
                s_ref[at, shared.stop : keys - PAGE] = s[:, shared.stop : keys - PAGE]
            s_ref[at, keys - PAGE : keys] = s[:, keys - PAGE :] + last_bias

        def weigh(t):
            at = slice(t % 2 * CHUNK, (t % 2 + 1) * CHUNK)
            s = s_ref[at, :keys]
            top = s[:, :HD]
            for n in range(1, keys // HD):
                top = jnp.maximum(top, s[:, n * HD : (n + 1) * HD])
            high = jnp.max(top, axis=1, keepdims=True) * to_exp2
            p = jnp.exp2(s * to_exp2 - high)
            mass = p[:, :HD]
            for n in range(1, keys // HD):
                mass = mass + p[:, n * HD : (n + 1) * HD]
            l_ref[at, :] = mass
            h_ref[at, :] = jnp.broadcast_to(high, (CHUNK, HD))
            p_ref[at, :keys] = p.astype(bf16)

        def send(n):
            return pltpu.make_async_copy(out_ref.at[n], out_hbm.at[:, (x + n) % NX], sems.at[n])

        def gather(t, levels):
            n, part = divmod(t, per_set)
            at = slice(t % 2 * CHUNK, (t % 2 + 1) * CHUNK)
            num = jnp.dot(p_ref[at, :keys], v_ref[:keys], preferred_element_type=f32)
            mass = jnp.sum(l_ref[at, :], axis=1, keepdims=True)
            done = (num / mass).astype(bf16)
            level = h_ref[at, :] + jnp.log2(mass)
            for m in range(CHUNK // PAGE):
                g = part * (CHUNK // PAGE) + m
                rows = slice(m * PAGE, (m + 1) * PAGE)
                out_ref[n, :, g * TOK : (g + 1) * TOK] = done[rows].reshape(KVH, TOK, HD)
                levels = jnp.where(lane == g, level[rows], levels)
            if part == per_set - 1:
                high = levels.astype(bf16).astype(f32)
                rest = levels - high
                middle = rest.astype(bf16).astype(f32)
                stats = high + pltpu.roll(middle, GROUP, 1) + pltpu.roll(rest - middle, 2 * GROUP, 1)
                out_ref[n, :, GROUP * TOK :] = stats.astype(bf16).reshape(KVH, TOK, HD)
                send(n).start()
            return levels

        levels = None
        for t in range(total + 2):
            if t >= 2:
                if (t - 2) % per_set == 0:
                    levels = jnp.zeros((PAGE, HD), f32)
                levels = gather(t - 2, levels)
            if t < total:
                score(t)
            if 1 <= t < total + 1:
                weigh(t - 1)
        for n in range(NX):
            send(n).wait()

    for rows in range(NY // 2):
        pl.when(y // 2 == rows)(lambda rows=rows: run(2 * rows + 1))


def combine(in_ref, out_ref):
    for h in range(KVH):
        levels = []
        for i in range(NX):
            pieces = in_ref[h * NX + i, GROUP * TOK :].astype(f32)
            levels.append(pieces + pltpu.roll(pieces, HD - GROUP, 1) + pltpu.roll(pieces, HD - 2 * GROUP, 1))
        top = jnp.maximum(jnp.maximum(levels[0], levels[1]), jnp.maximum(levels[2], levels[3]))
        shares = [jnp.exp2(v - top) for v in levels]
        whole = shares[0] + shares[1] + shares[2] + shares[3]
        shares = [v / whole for v in shares]
        for g in range(GROUP):
            done = jnp.zeros((TOK, HD), f32)
            for i in range(NX):
                part = in_ref[h * NX + i, g * TOK : (g + 1) * TOK].astype(f32)
                done = done + part * shares[i][:, g : g + 1]
            out_ref[:, h * QW + g * HD : h * QW + (g + 1) * HD] = done.astype(bf16)


def keep_pages(*refs):
    *ins, store_ref, scale_ref = refs

    def total(at):
        part = ins[0][at].astype(f32)
        for ref in ins[1:]:
            part = part + ref[at].astype(f32)
        return part

    for slot in range(SLOTS):
        store_ref[slot] = total(slice(slot * PAGE, (slot + 1) * PAGE)).astype(bf16)
    tops = total(slice(SLOTS * PAGE, SLOTS * PAGE + TOK))
    row = lax.broadcasted_iota(jnp.int32, (2, 2), 0)
    col = lax.broadcasted_iota(jnp.int32, (2, 2), 1)
    upper = jnp.where(col == 0, tops[:1, 0:1], tops[:1, 1:2])
    lower = jnp.where(col == 0, tops[:1, 2:3], tops[:1, 3:4])
    scale_ref[...] = jnp.where(row == 0, upper, lower).astype(bf16)


def on_device(queries, slab_kv, prefix_kv, owners, offset):
    y, x = lax.axis_index("y"), lax.axis_index("x")
    begin = offset[0]
    place = jnp.stack([y, x, begin]).astype(jnp.int32)

    packed = pl.pallas_call(
        pack,
        out_shape=shaped((KVH, TOK, QW + WIDE)),
        in_specs=[spec(SMEM), spec(pltpu.HBM), spec(pltpu.HBM)],
        out_specs=spec(),
        scratch_shapes=[VMEM((TOK, HQ * HD), bf16), VMEM((TOK, KVH * WIDE), bf16), pltpu.SemaphoreType.DMA((2,))],
        compiler_params=params(60),
        name="pack",
    )(offset, queries[0], slab_kv[0])
    grouped = lax.all_to_all(packed, "seq", 0, 0, tiled=True)

    kv_send, q_own = pl.pallas_call(
        spread,
        out_shape=(shaped((NY, PAGE + PRE, WIDE)), shaped((ROWS, HD))),
        in_specs=[spec(), spec()],
        out_specs=(spec(), spec()),
        compiler_params=params(),
        name="spread",
    )(grouped, prefix_kv)
    column = lax.all_to_all(kv_send, "y", 0, 0, tiled=True)
    asked = [q_own] + [lax.ppermute(q_own, "x", [(i, (i - k) % NX) for i in range(NX)]) for k in range(1, NX)]

    parts = pl.pallas_call(
        attend,
        out_shape=shaped((KVH, NX, MESSAGE, HD)),
        in_specs=[spec(SMEM)] + [spec()] * (1 + NX),
        out_specs=spec(pltpu.HBM),
        scratch_shapes=[
            VMEM((KEYS, HD), bf16),
            VMEM((KEYS, HD), bf16),
            VMEM((2 * CHUNK, KEYS), f32),
            VMEM((2 * CHUNK, KEYS), bf16),
            VMEM((2 * CHUNK, HD), f32),
            VMEM((2 * CHUNK, HD), f32),
            VMEM((NX, KVH, MESSAGE, HD), bf16),
            pltpu.SemaphoreType.DMA((NX,)),
        ],
        compiler_params=params(),
        cost_estimate=cost(4 * NX * ROWS * KEYS * HD, 4 << 20, NX * ROWS * KEYS),
        name="attend",
    )(place, column, *asked)
    parts = lax.all_to_all(parts.reshape(KVH * NX, MESSAGE, HD), ("seq", "x"), 0, 0, tiled=True)

    offered = pl.pallas_call(
        offer_pages,
        out_shape=(shaped((SLOTS * PAGE + TOK, WIDE)),) * NX,
        in_specs=[spec(SMEM), spec(SMEM), spec()],
        out_specs=(spec(),) * NX,
        compiler_params=params(),
        name="offer_pages",
    )(place, owners, column)
    delivered = [offered[0]] + [
        lax.ppermute(offered[k], "x", [(i, (i + k) % NX) for i in range(NX)]) for k in range(1, NX)
    ]
    stored, scales = pl.pallas_call(
        keep_pages,
        out_shape=(shaped((SLOTS, PAGE, WIDE)), shaped((2, 2))),
        in_specs=[spec()] * NX,
        out_specs=(spec(), spec()),
        compiler_params=params(),
        name="keep_pages",
    )(*delivered)
    attention = pl.pallas_call(
        combine,
        out_shape=shaped((TOK, HQ * HD)),
        in_specs=[spec()],
        out_specs=spec(),
        compiler_params=params(),
        name="combine",
    )(parts)
    return attention[None], stored[None, None], scales[None, None]


def solution(mesh):
    sizes = mesh.shape
    devices = mesh.devices.reshape(sizes["seq"], NY, NX, sizes["rep"])
    whole = Mesh(devices, ("seq", "y", "x", "rep"))
    dec = ("y", "x")
    return jax.shard_map(
        on_device,
        mesh=whole,
        in_specs=(
            P(("rep",) + dec, "seq", None),
            P(("rep",) + dec, "seq", None),
            P(("rep",) + dec, "seq"),
            P(("rep", "seq"), None),
            P("rep"),
        ),
        out_specs=(
            P(("rep",) + dec, "seq", None),
            P(("rep", "seq"), dec, None, None, None),
            P(("rep", "seq"), dec, None, None),
        ),
        check_vma=False,
    )
```

```python
import math

import jax
import jax.numpy as jnp
import numpy as np
from jax import lax
from jax.experimental import pallas as pl
from jax.experimental.pallas import tpu as pltpu
from jax.sharding import Mesh, PartitionSpec as P

HQ = 64
KVH = 8
HD = 128
PAGE = 128
GROUP = HQ // KVH
TOK = 16
WIDE = 2 * HD
QW = GROUP * HD
ROWS = GROUP * PAGE
NX = 4
NY = 8
PRE = 32
SLAB = NY * PAGE
KEYS = SLAB + NY * PRE
SLOTS = 2
CHUNK = 512
MESSAGE = (GROUP + 1) * TOK

rope_base = 1000000.0
tiny = 1e-06
masked = -1e30
to_exp2 = HD ** (-0.5) * math.log2(math.e)

VMEM = pltpu.VMEM
SMEM = pltpu.SMEM
f32 = jnp.float32
bf16 = jnp.bfloat16


def spec(space=VMEM):
    return pl.BlockSpec(memory_space=space)


def params(mib=32):
    return pltpu.CompilerParams(vmem_limit_bytes=mib * 1024 * 1024)


def cost(flops, moved, exps=0):
    return pl.CostEstimate(flops=flops, bytes_accessed=moved, transcendentals=exps)


def shaped(shape, dtype=bf16):
    return jax.ShapeDtypeStruct(shape, dtype)


def pack(offset_ref, q_hbm, kv_hbm, out_ref, q_ref, kv_ref, sems):
    block = lax.axis_index("y") * NX + lax.axis_index("x")
    first = offset_ref[0] + block * PAGE + lax.axis_index("seq") * TOK
    fetch_q = pltpu.make_async_copy(q_hbm, q_ref, sems.at[0])
    fetch_kv = pltpu.make_async_copy(kv_hbm, kv_ref, sems.at[1])
    fetch_q.start()
    fetch_kv.start()
    half = HD // 2
    lane = lax.broadcasted_iota(jnp.int32, (TOK, HD), 1)
    place = lane % half
    inverse = jnp.zeros((TOK, HD), f32)
    for k in range(half):
        inverse = jnp.where(place == k, float(np.float32(rope_base ** (-2.0 * k / HD))), inverse)
    row = lax.broadcasted_iota(jnp.int32, (TOK, HD), 0) + first
    angles = row.astype(f32) * inverse
    cosine = jnp.cos(angles)
    sinus = jnp.sin(angles)
    sinus = jnp.where(lane < half, -sinus, sinus)

    def turn(x):
        x = x.astype(f32)
        return (x * cosine + pltpu.roll(x, half, 1) * sinus).astype(bf16)

    fetch_kv.wait()
    for h in range(KVH):
        out_ref[h, :, QW : QW + HD] = turn(kv_ref[:, h * WIDE : h * WIDE + HD])
        out_ref[h, :, QW + HD :] = kv_ref[:, h * WIDE + HD : (h + 1) * WIDE]
    fetch_q.wait()
    for h in range(KVH):
        for g in range(GROUP):
            q = h * GROUP + g
            out_ref[h, :, g * HD : (g + 1) * HD] = turn(q_ref[:, q * HD : (q + 1) * HD])


def spread(in_ref, pre_ref, kv_ref, q_ref):
    own = in_ref[:, :, QW:].reshape(PAGE, WIDE)
    pre = pre_ref[...]
    for j in range(NY):
        kv_ref[j, :PAGE] = own
        kv_ref[j, PAGE:] = pre
    for g in range(GROUP):
        q_ref[g * PAGE : (g + 1) * PAGE] = in_ref[:, :, g * HD : (g + 1) * HD].reshape(PAGE, HD)


def offer_pages(place_ref, own_ref, col_ref, *outs):
    y, x = place_ref[0], place_ref[1]
    pages = own_ref.shape[1]
    found = [[jnp.int32(pages)] * SLOTS for _ in range(NX)]
    owners = [y * NX + (x + k) % NX for k in range(NX)]
    for p in reversed(range(pages)):
        for k in range(NX):
            hit = own_ref[0, p] == owners[k]
            one, two = found[k]
            found[k] = [jnp.where(hit, p, one), jnp.where(hit, one, two)]
    lane = lax.broadcasted_iota(jnp.int32, (TOK, WIDE), 1)
    for k in range(NX):
        tops = jnp.zeros((TOK, WIDE), f32)
        for slot in range(SLOTS):
            page = found[k][slot]
            held = jnp.where((page < pages) & (page % NX == x), 1.0, 0.0)
            row = jnp.minimum(page // NX, NY - 1)
            for half in range(2):
                part = col_ref[row, :PAGE, half * HD : (half + 1) * HD].astype(f32)
                top = jnp.max(jnp.max(jnp.abs(part), axis=0, keepdims=True), axis=1, keepdims=True)
                scaled = part * (held / (top + tiny))
                outs[k][slot * PAGE : (slot + 1) * PAGE, half * HD : (half + 1) * HD] = scaled.astype(bf16)
                tops = jnp.where(lane == slot * 2 + half, top * held, tops)
        outs[k][SLOTS * PAGE :] = tops.astype(bf16)


def attend(place_ref, col_ref, *refs):
    *queries, out_hbm, k_ref, v_ref, s_ref, p_ref, l_ref, h_ref, out_ref, sems = refs
    y, x, begin = place_ref[0], place_ref[1], place_ref[2]
    for at, j in [(0, 0)] + [(PAGE + NY * PRE + (j - 1) * PAGE, j) for j in range(1, NY)]:
        b = (y - j + NY) % NY
        k_ref[at : at + PAGE] = col_ref[b, :PAGE, :HD]
        v_ref[at : at + PAGE] = col_ref[b, :PAGE, HD:]
    shared = slice(PAGE, PAGE + NY * PRE)
    k_ref[shared] = col_ref[:, PAGE:, :HD].reshape(NY * PRE, HD)
    v_ref[shared] = col_ref[:, PAGE:, HD:].reshape(NY * PRE, HD)

    always = slice(PAGE, 2 * PAGE)
    perhaps = slice(2 * PAGE, PAGE + NY * PRE)
    i = lax.broadcasted_iota(jnp.int32, (1, NY * PRE - PAGE), 1) + PAGE
    prefix_bias = jnp.where(((i // PRE) * NX + x) * PRE + i % PRE < begin, 0.0, masked)
    token = lax.broadcasted_iota(jnp.int32, (CHUNK, PAGE), 0) % PAGE
    own_key = lax.broadcasted_iota(jnp.int32, (CHUNK, PAGE), 1)
    lane = lax.broadcasted_iota(jnp.int32, (PAGE, HD), 1)
    per_set = ROWS // CHUNK
    total = NX * per_set

    def run(blocks):
        keys = PAGE + NY * PRE + blocks * PAGE
        last_bias = jnp.where(y >= blocks, 0.0, masked)

        def score(t):
            n, part = divmod(t, per_set)
            q = queries[n][part * CHUNK : (part + 1) * CHUNK]
            s = lax.dot_general(q, k_ref[:keys], (((1,), (1,)), ((), ())), preferred_element_type=f32)
            at = slice(t % 2 * CHUNK, (t % 2 + 1) * CHUNK)
            if n == 0:
                s_ref[at, :PAGE] = jnp.where(own_key <= token, s[:, :PAGE], masked)
            else:
                s_ref[at, :PAGE] = s[:, :PAGE] + jnp.where((x + n) % NX > x, 0.0, masked)
            s_ref[at, always] = s[:, always]
            s_ref[at, perhaps] = s[:, perhaps] + prefix_bias
            if blocks > 1:
                s_ref[at, shared.stop : keys - PAGE] = s[:, shared.stop : keys - PAGE]
            s_ref[at, keys - PAGE : keys] = s[:, keys - PAGE :] + last_bias

        def weigh(t):
            at = slice(t % 2 * CHUNK, (t % 2 + 1) * CHUNK)
            s = s_ref[at, :keys]
            top = s[:, :HD]
            for n in range(1, keys // HD):
                top = jnp.maximum(top, s[:, n * HD : (n + 1) * HD])
            high = jnp.max(top, axis=1, keepdims=True) * to_exp2
            p = jnp.exp2(s * to_exp2 - high)
            mass = p[:, :HD]
            for n in range(1, keys // HD):
                mass = mass + p[:, n * HD : (n + 1) * HD]
            l_ref[at, :] = mass
            h_ref[at, :] = jnp.broadcast_to(high, (CHUNK, HD))
            p_ref[at, :keys] = p.astype(bf16)

        def send(n):
            return pltpu.make_async_copy(out_ref.at[n], out_hbm.at[:, (x + n) % NX], sems.at[n])

        def gather(t, levels):
            n, part = divmod(t, per_set)
            at = slice(t % 2 * CHUNK, (t % 2 + 1) * CHUNK)
            num = jnp.dot(p_ref[at, :keys], v_ref[:keys], preferred_element_type=f32)
            mass = jnp.sum(l_ref[at, :], axis=1, keepdims=True)
            done = (num / mass).astype(bf16)
            level = h_ref[at, :] + jnp.log2(mass)
            for m in range(CHUNK // PAGE):
                g = part * (CHUNK // PAGE) + m
                rows = slice(m * PAGE, (m + 1) * PAGE)
                out_ref[n, :, g * TOK : (g + 1) * TOK] = done[rows].reshape(KVH, TOK, HD)
                levels = jnp.where(lane == g, level[rows], levels)
            if part == per_set - 1:
                high = levels.astype(bf16).astype(f32)
                rest = levels - high
                middle = rest.astype(bf16).astype(f32)
                stats = high + pltpu.roll(middle, GROUP, 1) + pltpu.roll(rest - middle, 2 * GROUP, 1)
                out_ref[n, :, GROUP * TOK :] = stats.astype(bf16).reshape(KVH, TOK, HD)
                send(n).start()
            return levels

        levels = None
        for t in range(total + 2):
            if t >= 2:
                if (t - 2) % per_set == 0:
                    levels = jnp.zeros((PAGE, HD), f32)
                levels = gather(t - 2, levels)
            if t < total:
                score(t)
            if 1 <= t < total + 1:
                weigh(t - 1)
        for n in range(NX):
            send(n).wait()

    for rows in range(NY // 2):
        pl.when(y // 2 == rows)(lambda rows=rows: run(2 * rows + 1))


def combine(in_ref, out_ref):
    for h in range(KVH):
        levels = []
        for i in range(NX):
            pieces = in_ref[h * NX + i, GROUP * TOK :].astype(f32)
            levels.append(pieces + pltpu.roll(pieces, HD - GROUP, 1) + pltpu.roll(pieces, HD - 2 * GROUP, 1))
        top = jnp.maximum(jnp.maximum(levels[0], levels[1]), jnp.maximum(levels[2], levels[3]))
        shares = [jnp.exp2(v - top) for v in levels]
        whole = shares[0] + shares[1] + shares[2] + shares[3]
        shares = [v / whole for v in shares]
        for g in range(GROUP):
            done = jnp.zeros((TOK, HD), f32)
            for i in range(NX):
                part = in_ref[h * NX + i, g * TOK : (g + 1) * TOK].astype(f32)
                done = done + part * shares[i][:, g : g + 1]
            out_ref[:, h * QW + g * HD : h * QW + (g + 1) * HD] = done.astype(bf16)


def keep_pages(*refs):
    *ins, store_ref, scale_ref = refs

    def total(at):
        part = ins[0][at].astype(f32)
        for ref in ins[1:]:
            part = part + ref[at].astype(f32)
        return part

    for slot in range(SLOTS):
        store_ref[slot] = total(slice(slot * PAGE, (slot + 1) * PAGE)).astype(bf16)
    tops = total(slice(SLOTS * PAGE, SLOTS * PAGE + TOK))
    row = lax.broadcasted_iota(jnp.int32, (2, 2), 0)
    col = lax.broadcasted_iota(jnp.int32, (2, 2), 1)
    upper = jnp.where(col == 0, tops[:1, 0:1], tops[:1, 1:2])
    lower = jnp.where(col == 0, tops[:1, 2:3], tops[:1, 3:4])
    scale_ref[...] = jnp.where(row == 0, upper, lower).astype(bf16)


def on_device(queries, slab_kv, prefix_kv, owners, offset):
    y, x = lax.axis_index("y"), lax.axis_index("x")
    begin = offset[0]
    place = jnp.stack([y, x, begin]).astype(jnp.int32)

    packed = pl.pallas_call(
        pack,
        out_shape=shaped((KVH, TOK, QW + WIDE)),
        in_specs=[spec(SMEM), spec(pltpu.HBM), spec(pltpu.HBM)],
        out_specs=spec(),
        scratch_shapes=[VMEM((TOK, HQ * HD), bf16), VMEM((TOK, KVH * WIDE), bf16), pltpu.SemaphoreType.DMA((2,))],
        compiler_params=params(60),
        name="pack",
    )(offset, queries[0], slab_kv[0])
    grouped = lax.all_to_all(packed, "seq", 0, 0, tiled=True)

    kv_send, q_own = pl.pallas_call(
        spread,
        out_shape=(shaped((NY, PAGE + PRE, WIDE)), shaped((ROWS, HD))),
        in_specs=[spec(), spec()],
        out_specs=(spec(), spec()),
        compiler_params=params(),
        name="spread",
    )(grouped, prefix_kv)
    column = lax.all_to_all(kv_send, "y", 0, 0, tiled=True)
    asked = [q_own] + [lax.ppermute(q_own, "x", [(i, (i - k) % NX) for i in range(NX)]) for k in range(1, NX)]

    parts = pl.pallas_call(
        attend,
        out_shape=shaped((KVH, NX, MESSAGE, HD)),
        in_specs=[spec(SMEM)] + [spec()] * (1 + NX),
        out_specs=spec(pltpu.HBM),
        scratch_shapes=[
            VMEM((KEYS, HD), bf16),
            VMEM((KEYS, HD), bf16),
            VMEM((2 * CHUNK, KEYS), f32),
            VMEM((2 * CHUNK, KEYS), bf16),
            VMEM((2 * CHUNK, HD), f32),
            VMEM((2 * CHUNK, HD), f32),
            VMEM((NX, KVH, MESSAGE, HD), bf16),
            pltpu.SemaphoreType.DMA((NX,)),
        ],
        compiler_params=params(),
        cost_estimate=cost(4 * NX * ROWS * KEYS * HD, 4 << 20, NX * ROWS * KEYS),
        name="attend",
    )(place, column, *asked)
    parts = lax.all_to_all(parts.reshape(KVH * NX, MESSAGE, HD), ("seq", "x"), 0, 0, tiled=True)

    offered = pl.pallas_call(
        offer_pages,
        out_shape=(shaped((SLOTS * PAGE + TOK, WIDE)),) * NX,
        in_specs=[spec(SMEM), spec(SMEM), spec()],
        out_specs=(spec(),) * NX,
        compiler_params=params(),
        name="offer_pages",
    )(place, owners, column)
    delivered = [offered[0]] + [
        lax.ppermute(offered[k], "x", [(i, (i + k) % NX) for i in range(NX)]) for k in range(1, NX)
    ]
    stored, scales = pl.pallas_call(
        keep_pages,
        out_shape=(shaped((SLOTS, PAGE, WIDE)), shaped((2, 2))),
        in_specs=[spec()] * NX,
        out_specs=(spec(), spec()),
        compiler_params=params(),
        name="keep_pages",
    )(*delivered)
    attention = pl.pallas_call(
        combine,
        out_shape=shaped((TOK, HQ * HD)),
        in_specs=[spec()],
        out_specs=spec(),
        compiler_params=params(),
        name="combine",
    )(parts)
    return attention[None], stored[None, None], scales[None, None]


def solution(mesh):
    sizes = mesh.shape
    devices = mesh.devices.reshape(sizes["seq"], NY, NX, sizes["rep"])
    whole = Mesh(devices, ("seq", "y", "x", "rep"))
    dec = ("y", "x")
    return jax.shard_map(
        on_device,
        mesh=whole,
        in_specs=(
            P(("rep",) + dec, "seq", None),
            P(("rep",) + dec, "seq", None),
            P(("rep",) + dec, "seq"),
            P(("rep", "seq"), None),
            P("rep"),
        ),
        out_specs=(
            P(("rep",) + dec, "seq", None),
            P(("rep", "seq"), dec, None, None, None),
            P(("rep", "seq"), dec, None, None),
        ),
        check_vma=False,
    )
```
